32 devices in a mesh: obs: 2 (over x), chan: 16 (over z, y, core).
Axes of the slice: x: 2, y: 2, z: 4, core: 2. Of those that a mesh axis runs over, the one named last changes fastest.
Arguments:
- visibilities: bfloat16 [2, 8192, 384], P(None, ('obs', 'chan')), parts along dimension 1, may hold values from -6 to 6
- kernel: bfloat16 [4, 8192, 128], P(None, ('obs', 'chan')), parts along dimension 1, may hold values from -0.09375 to 0.09375
- weights: int32 [8192], P(('obs', 'chan')), parts along dimension 0, may hold values from 1 to 4
- counts: int32 [8192], P(('obs', 'chan')), parts along dimension 0, may hold values from 1 to 4, as said below
- blocks: int32 [4, 8192], P(None, ('obs', 'chan')), parts along dimension 1, may hold values from 0 to 15, as said below
- inv_cov: bfloat16 [384, 384], replicated, as said below
Outputs:
- delay_cube: float32 [2, 384, 4096], P(None, None, ('obs', 'chan')), parts along dimension 2
The draws below stay inside these ranges and needn't reach their ends.
There are 2 independent parts, one for each index of `obs`. The reference program is written for one: setup_inputs(seed, part) draws one part's arguments, and reference() takes and returns one part's arrays. A program takes and returns all parts, laid end to end along the dimension named above; an argument that names none is the same for every part. Nothing has to cross between parts.
Inputs may be any that keep to these rules, and one draw needn't show every extreme that they name: Each sample's used blocks are the first counts of its list; the most is reached in every draw. `blocks`: row j of a sample's list is its row 0 plus j modulo 16. In each aligned group of 16 samples, row 0 holds every block number exactly once. `inv_cov`: Symmetric.
All inputs are finite; a program needn't handle non-finite values.
Results may differ from the reference program's by a relative error of at most 0.0049.
Values may be sent and summed in bfloat16 or wider, within the bound.
No kernel may reach another device: no remote copies, remote signals or barrier semaphores. Data moves between devices by JAX's collectives and lax.ppermute only.
A program may use at most 256 MiB of HBM per device.

```python
import math
import jax
import jax.numpy as jnp

NCH = 384
MAXB = 4
SAMP_DEV = 256
CELLS_DEV = 128
SAMPLES = 4096
NBLK = 16


def draw_counts(key, part):
    key = jax.random.fold_in(key, 11)
    first, second = jax.random.split(key)
    cell_groups = SAMPLES // SAMP_DEV
    level = jax.random.randint(first, (cell_groups,), 0, MAXB)
    spread_kernel = jnp.repeat(level, SAMP_DEV)
    extra = jax.random.randint(second, (SAMPLES,), 0, MAXB)
    result = 1 + jnp.minimum(extra, spread_kernel)
    result = result.at[0].set(MAXB).at[1].set(1)
    return result.astype(jnp.int32)


def draw_blocks(key, part):
    key = jax.random.fold_in(key, 12)
    cell_groups = SAMPLES // NBLK
    scores = jax.random.randint(key, (cell_groups, NBLK), 0, 1048576) * NBLK + jnp.arange(NBLK, dtype=jnp.int32)[None, :]
    start = jnp.argsort(scores, axis=1, stable=True).astype(jnp.int32).reshape(SAMPLES)
    listed = (start[None, :] + jnp.arange(MAXB, dtype=jnp.int32)[:, None]) % NBLK
    return listed.astype(jnp.int32)


def draw_inv_cov(key, part):
    key = jax.random.fold_in(key, 13)
    base = jax.random.normal(key, (NCH, NCH), jnp.float32)
    symmetric = (base + base.T) * (0.5 / jnp.sqrt(jnp.float32(NCH)))
    return (symmetric + jnp.eye(NCH, dtype=jnp.float32)).astype(jnp.bfloat16)


def with_ends(values, rng, low, high):
    spot = [jax.random.randint(jax.random.fold_in(rng, axis), (), 0, length) for axis, length in enumerate(values.shape)]
    widest = values.shape.index(max(values.shape))
    neighbour = spot[:widest] + [(spot[widest] + 1) % values.shape[widest]] + spot[widest + 1:]
    return values.at[tuple(spot)].set(low).at[tuple(neighbour)].set(high)


def with_spikes(values, key, source, target, parts, factor):
    def block_of(axis_at):
        return (jnp.arange(values.shape[axis_at]) // (values.shape[axis_at] // parts)).reshape((-1,) + (1,) * (values.ndim - 1 - axis_at))

    near = jax.random.permutation(key, parts)[block_of(target)]
    far = (block_of(target) + parts // 2) % parts
    return jnp.where((block_of(source) == near) | (block_of(source) == far), factor * values, values)


def level_of(own_key, dims, shards, smallest, high):
    def one(position, blocks):
        steps = jax.random.uniform(jax.random.fold_in(jax.random.fold_in(own_key, 6), position), (blocks,), jnp.float32, smallest / len(shards), high / len(shards))
        return jnp.repeat(jnp.exp(steps), dims[position] // blocks).reshape((-1,) + (1,) * (len(dims) - position - 1))

    factor_of = one(*shards[0])
    for cut in shards[1:]:
        factor_of = factor_of * one(*cut)
    return factor_of


def gaussian(own_key, extent, spread, reach, cuts=(), held_as=jnp.bfloat16):
    array = spread * jax.random.normal(own_key, extent, jnp.float32)
    if cuts:
        array = array * level_of(own_key, extent, cuts, -0.22, 0.18)
    return jnp.clip(array, -reach, reach).astype(held_as)


def heavy_noise(stream_key, extent, spread, most, cuts, heavy, kind=jnp.bfloat16):
    drawn = spread * jax.random.normal(stream_key, extent, jnp.float32)
    if cuts:
        drawn = drawn * level_of(stream_key, extent, cuts, -0.22, 0.18)
    return jnp.clip(with_spikes(drawn, jax.random.fold_in(stream_key, 3), *heavy), -most, most).astype(kind)


def setup_inputs(seed: int = 0, part: int = 0) -> dict:
    key_list = jax.random.split(jax.random.key(seed), 7)
    part_keys = jax.random.split(jax.random.fold_in(key_list[6], part), 7)
    visibilities = heavy_noise(part_keys[0], (2, SAMPLES, NCH), 1.0, 6.0, ((1, 16),), (1, 2, 16, 2.0))
    kernel = gaussian(part_keys[1], (MAXB, SAMPLES, CELLS_DEV), (SAMP_DEV * MAXB * 4) ** -0.5, 0.09375, ((1, 16),))
    weights = with_ends(jax.random.randint(part_keys[2], (SAMPLES,), 1, 5), jax.random.fold_in(part_keys[2], 1), 1, 4).astype(jnp.int32)
    counts = draw_counts(jax.random.fold_in(jax.random.fold_in(key_list[6], part), 71), part)
    blocks = draw_blocks(jax.random.fold_in(jax.random.fold_in(key_list[6], part), 71), part)
    inv_cov = draw_inv_cov(jax.random.fold_in(key_list[6], 71), part)
    return {"visibilities": visibilities, "kernel": kernel, "weights": weights, "counts": counts, "blocks": blocks, "inv_cov": inv_cov}


def weigh_kernel(kernel, weights, counts):
    live = jnp.arange(MAXB, dtype=jnp.int32)[:, None] < counts[None, :]
    scaled = kernel.astype(jnp.float32) * weights.astype(jnp.float32)[None, :, None]
    return jnp.where(live[:, :, None], scaled, jnp.zeros_like(scaled)).astype(jnp.bfloat16)

def grid_samples(vis_rows, weighted, starts):
    ranking = jnp.argsort(starts, stable=True).astype(jnp.int32)
    group_rows = starts.shape[0] // NBLK
    sorted_rows = jnp.take(vis_rows, ranking, axis=1).reshape(vis_rows.shape[0], NBLK, group_rows).astype(jnp.float32)
    sorted_kernel = jnp.take(weighted, ranking, axis=1).reshape(MAXB, NBLK, group_rows, CELLS_DEV).astype(jnp.float32)
    summed = jnp.zeros((vis_rows.shape[0], NBLK, CELLS_DEV), jnp.float32)
    for offset in range(MAXB):
        placed = jnp.einsum('cts,tsk->ctk', sorted_rows, sorted_kernel[offset])
        summed = summed + jnp.roll(placed, offset, axis=1)
    return summed.reshape(vis_rows.shape[0], NBLK * CELLS_DEV)

def delay_transform(cube, inv_cov):
    filtered = jnp.einsum('gh,chn->cgn', inv_cov.astype(jnp.float32), cube.astype(jnp.float32)).astype(jnp.bfloat16)
    index = jnp.arange(NCH, dtype=jnp.int32)
    product = index[:, None] * index[None, :] % NCH
    angle = product.astype(jnp.float32) * (2.0 * math.pi / NCH)
    cosine_lookup = jnp.cos(angle).astype(jnp.bfloat16)
    sin_table = jnp.sin(angle).astype(jnp.bfloat16)
    real_part = jnp.dot(cosine_lookup, filtered[0], preferred_element_type=jnp.float32) + jnp.dot(sin_table, filtered[1], preferred_element_type=jnp.float32)
    imag_part = jnp.dot(cosine_lookup, filtered[1], preferred_element_type=jnp.float32) - jnp.dot(sin_table, filtered[0], preferred_element_type=jnp.float32)
    return jnp.stack([real_part, imag_part]) * (1.0 / math.sqrt(NCH))

def reference(visibilities, kernel, weights, counts, blocks, inv_cov):
    weighted = weigh_kernel(kernel, weights, counts)
    vis_rows = visibilities.transpose(0, 2, 1).reshape(2 * NCH, SAMPLES)
    grid = grid_samples(vis_rows, weighted, blocks[0]).reshape(2, NCH, NBLK * CELLS_DEV)
    cube = grid.astype(jnp.bfloat16)
    return delay_transform(cube, inv_cov)
```

```python
import math

import jax
import jax.numpy as jnp
import numpy as np
from jax import lax
from jax.experimental import pallas as pl
from jax.experimental.pallas import tpu as pltpu
from jax.sharding import PartitionSpec as P

MAXB = 4
LABEL_ROWS = 16
CHUNK = 128
VMEM_BYTES = 48 * 1024 * 1024


def delay_tables(channels):
    index = np.arange(channels, dtype=np.int64)
    product = index[:, None] * index[None, :] % channels
    angle = product.astype(np.float32) * np.float32(2.0 * math.pi / channels)
    return jnp.asarray(np.cos(angle).astype(jnp.bfloat16)), jnp.asarray(
        np.sin(angle).astype(jnp.bfloat16)
    )


def prep_body(nblocks, nchunks, vis, kernel, weights, counts, blocks, own, core, far, *chunks):
    cells = kernel.shape[2]
    me = lax.axis_index("chan")
    start = blocks[0:1, :]
    weight = weights[...].reshape(1, -1).astype(jnp.float32)
    count = counts[...].reshape(1, -1)
    turned = [kernel[j].astype(jnp.float32).T for j in range(MAXB)]

    def pick(flip):
        residue = jnp.bitwise_xor(jnp.bitwise_and(me, MAXB - 1), flip)
        which = jnp.bitwise_and(residue - start, MAXB - 1)
        total = None
        for j in range(MAXB):
            gain = jnp.where((which == j) & (j < count), weight, 0.0)
            term = turned[j] * gain
            total = term if total is None else total + term
        label = lax.rem(start + which, nblocks) // MAXB
        return total.astype(jnp.bfloat16), jnp.broadcast_to(
            label.astype(jnp.float32), (LABEL_ROWS, start.shape[1])
        ).astype(jnp.bfloat16)

    own[:cells, :], own[cells:, :] = pick(0)
    core[:cells, :], core[cells:, :] = pick(1)
    far[:cells, :], far[2 * cells : 2 * cells + LABEL_ROWS, :] = pick(2)
    far[cells : 2 * cells, :], far[2 * cells + LABEL_ROWS :, :] = pick(3)
    for k in range(nchunks):
        for part in range(2):
            chunks[k][:, part * CHUNK : (part + 1) * CHUNK] = vis[
                part, :, k * CHUNK : (k + 1) * CHUNK
            ]


def grid_body(groups, k, own, core, far, relay, vis, vis_core, vis_far, vis_relay, send, keep, place, rows):
    samples = own.shape[1]
    cells = own.shape[0] - LABEL_ROWS
    me = lax.axis_index("chan")
    bit = jnp.bitwise_and(me // MAXB, 1).astype(jnp.float32)
    for part in range(2):
        lanes = slice(part * CHUNK, (part + 1) * CHUNK)
        rows[:samples, lanes] = vis[part, :, k * CHUNK : (k + 1) * CHUNK]
        rows[samples : 2 * samples, lanes] = vis_core[part, :, k * CHUNK : (k + 1) * CHUNK]
    rows[2 * samples : 3 * samples, :] = vis_far[...]
    rows[3 * samples :, :] = vis_relay[...]
    table = [
        (own[:cells, :], own[cells : cells + 1, :]),
        (core[:cells, :], core[cells : cells + 1, :]),
        (far[:cells, :], far[2 * cells : 2 * cells + 1, :]),
        (
            relay[cells : 2 * cells, :],
            relay[2 * cells + LABEL_ROWS : 2 * cells + LABEL_ROWS + 1, :],
        ),
    ]
    half = groups // 2
    for side in range(2):
        for p in range(half):
            wanted = 2.0 * p + (bit if side else 1.0 - bit)
            for source, (values, label) in enumerate(table):
                gain = jnp.where(label.astype(jnp.float32) == wanted, 1.0, 0.0).astype(jnp.bfloat16)
                place[
                    (side * half + p) * cells : (side * half + p + 1) * cells,
                    source * samples : (source + 1) * samples,
                ] = values * gain
        placed = jnp.dot(
            place[side * half * cells : (side + 1) * half * cells, :],
            rows[...],
            preferred_element_type=jnp.float32,
        ).reshape(half, cells, 2 * CHUNK)
        if side:
            keep[...] = placed
        else:
            send[...] = placed.astype(jnp.bfloat16)


def final_body(nchunks, *refs):
    kept, got = refs[:nchunks], refs[nchunks : 2 * nchunks]
    inv_cov, cos_table, sin_table, out = refs[2 * nchunks :]
    cells = out.shape[2]
    parts = []
    sums = [
        (kept[k][...] + got[k][...].astype(jnp.float32)).astype(jnp.bfloat16)
        for k in range(nchunks)
    ]
    for part in range(2):
        parts.append(
            jnp.concatenate(
                [s[:, part * CHUNK : (part + 1) * CHUNK] for s in sums], axis=1
            )
        )
    cube = jnp.concatenate(parts, axis=0)
    filtered = lax.dot_general(
        cube, inv_cov[...], (((1,), (1,)), ((), ())), preferred_element_type=jnp.float32
    ).astype(jnp.bfloat16)
    contract = (((1,), (1,)), ((), ()))
    cosine = lax.dot_general(cos_table[...], filtered, contract, preferred_element_type=jnp.float32)
    sine = lax.dot_general(sin_table[...], filtered, contract, preferred_element_type=jnp.float32)
    scale = 1.0 / math.sqrt(inv_cov.shape[0])
    out[0] = (cosine[:, :cells] + sine[:, cells:]) * scale
    out[1] = (cosine[:, cells:] - sine[:, :cells]) * scale


def on_device(visibilities, kernel, weights, counts, blocks, inv_cov):
    nblocks = lax.axis_size("chan")
    groups = nblocks // MAXB
    samples, channels = visibilities.shape[1:]
    cells = kernel.shape[2]
    nchunks = channels // CHUNK
    params = pltpu.CompilerParams(vmem_limit_bytes=VMEM_BYTES)
    bf16, f32 = jnp.bfloat16, jnp.float32
    shape = jax.ShapeDtypeStruct

    def swap(values, bit):
        return lax.ppermute(values, "chan", [(i, i ^ bit) for i in range(nblocks)])

    vis_core = swap(visibilities, 1)
    own, core, far, *chunks = pl.pallas_call(
        lambda *refs: prep_body(nblocks, nchunks, *refs),
        out_shape=[
            shape((cells + LABEL_ROWS, samples), bf16),
            shape((cells + LABEL_ROWS, samples), bf16),
            shape((2 * (cells + LABEL_ROWS), samples), bf16),
        ]
        + [shape((samples, 2 * CHUNK), bf16)] * nchunks,
        compiler_params=params,
        name="prep",
    )(visibilities, kernel, weights, counts, blocks)
    core = swap(core, 1)
    far = swap(far, 2)
    relay = swap(far, 1)
    me = lax.axis_index("chan")
    kept, got = [], []
    for k in range(nchunks):
        vis_far = swap(chunks[k], 2)
        vis_relay = swap(vis_far, 1)
        send, keep = pl.pallas_call(
            lambda *refs, k=k: grid_body(groups, k, *refs),
            out_shape=[
                shape((groups // 2, cells, 2 * CHUNK), bf16),
                shape((groups // 2, cells, 2 * CHUNK), f32),
            ],
            scratch_shapes=[
                pltpu.VMEM((groups * cells, MAXB * samples), bf16),
                pltpu.VMEM((MAXB * samples, 2 * CHUNK), bf16),
            ],
            compiler_params=params,
            name="grid",
        )(own, core, far, relay, visibilities, vis_core, vis_far, vis_relay)
        bit = MAXB
        while True:
            arrived = swap(send, bit)
            if keep.shape[0] == 1:
                break
            bit *= 2
            summed = (keep + arrived.astype(f32)).reshape(-1, 2, cells, 2 * CHUNK)
            upper = (me // bit) % 2 == 1
            keep = jnp.where(upper, summed[:, 1], summed[:, 0])
            send = jnp.where(upper, summed[:, 0], summed[:, 1]).astype(bf16)
        kept.append(keep[0])
        got.append(arrived[0])
    cos_table, sin_table = delay_tables(channels)
    return pl.pallas_call(
        lambda *refs: final_body(nchunks, *refs),
        out_shape=shape((2, channels, cells), f32),
        compiler_params=params,
        name="transform",
    )(*kept, *got, inv_cov, cos_table, sin_table)


def solution(mesh):
    placed = (
        P(None, ("obs", "chan"), None),
        P(None, ("obs", "chan"), None),
        P(("obs", "chan")),
        P(("obs", "chan")),
        P(None, ("obs", "chan")),
        P(),
    )
    return jax.shard_map(
        on_device,
        mesh=mesh,
        in_specs=placed,
        out_specs=P(None, None, ("obs", "chan")),
        check_vma=False,
    )
```

```python
import math

import jax
import jax.numpy as jnp
import numpy as np
from jax import lax
from jax.experimental import pallas as pl
from jax.experimental.pallas import tpu as pltpu
from jax.sharding import PartitionSpec as P

MAXB = 4
LABEL_ROWS = 16
CHUNK = 128
FIRST = ()
LATER = ((0, 1), (2, 3), (4, 5))
VMEM_BYTES = 48 * 1024 * 1024


def delay_tables(channels):
    index = np.arange(channels, dtype=np.int64)
    product = index[:, None] * index[None, :] % channels
    angle = product.astype(np.float32) * np.float32(2.0 * math.pi / channels)
    return jnp.asarray(np.cos(angle).astype(jnp.bfloat16)), jnp.asarray(
        np.sin(angle).astype(jnp.bfloat16)
    )


def unit(vis, u):
    return vis.at[u % 2, :, pl.ds(u // 2 * CHUNK, CHUNK)]


def prep_body(
    nblocks, plan, vis, kernel_in, weights_in, counts_in, blocks_in, own, core, far, *refs
):
    chunks, (kernel, weights, counts, blocks, sems, cut_sems) = refs[: len(plan)], refs[len(plan) :]
    copies = [
        pltpu.make_async_copy(source, target, sems.at[i])
        for i, (source, target) in enumerate(
            [(weights_in, weights), (counts_in, counts), (blocks_in, blocks), (kernel_in, kernel)]
        )
    ]
    cuts = [
        pltpu.make_async_copy(unit(vis, u), chunk.at[:, pl.ds(i * CHUNK, CHUNK)], cut_sems.at[u])
        for units, chunk in zip(plan, chunks)
        for i, u in enumerate(units)
    ]
    for copy in copies + cuts:
        copy.start()
    for copy in copies:
        copy.wait()
    cells = kernel.shape[2]
    me = lax.axis_index("chan")
    start = blocks[0:1, :]
    weight = weights[...].reshape(1, -1).astype(jnp.float32)
    count = counts[...].reshape(1, -1)
    turned = [kernel[j].astype(jnp.float32).T for j in range(MAXB)]
    picked = []
    for flip in range(MAXB):
        residue = jnp.bitwise_xor(jnp.bitwise_and(me, MAXB - 1), flip)
        which = jnp.bitwise_and(residue - start, MAXB - 1)
        total = None
        for j in range(MAXB):
            gain = jnp.where((which == j) & (j < count), weight, 0.0)
            term = turned[j] * gain
            total = term if total is None else total + term
        label = lax.rem(start + which, nblocks) // MAXB
        picked.append(
            (
                total.astype(jnp.bfloat16),
                jnp.broadcast_to(
                    label.astype(jnp.float32), (LABEL_ROWS, start.shape[1])
                ).astype(jnp.bfloat16),
            )
        )
    for out, flips in ((own, (0, 2)), (core, (1, 3)), (far, (2, 3))):
        for i, flip in enumerate(flips):
            out[i * cells : (i + 1) * cells, :] = picked[flip][0]
            out[2 * cells + i * LABEL_ROWS : 2 * cells + (i + 1) * LABEL_ROWS, :] = picked[flip][1]
    for copy in cuts:
        copy.wait()


def listed(table, i, cells):
    row = 2 * cells + i * LABEL_ROWS
    return table[i * cells : (i + 1) * cells, :], table[row : row + 1, :].astype(jnp.float32)


def place_and_sum(classes, groups, place, rows, send, keep):
    cells = send.shape[2]
    samples = classes[0][0][0].shape[1]
    half = groups // 2
    me = lax.axis_index("chan")
    bit = jnp.bitwise_and(me // MAXB, 1).astype(jnp.float32)
    for side, out in enumerate((send, keep)):
        for c, table in enumerate(classes):
            first = (side * len(classes) + c) * half * cells
            for p in range(half):
                wanted = 2.0 * p + (bit if side else 1.0 - bit)
                for source, (values, label) in enumerate(table):
                    gain = jnp.where(label == wanted, 1.0, 0.0).astype(jnp.bfloat16)
                    place[
                        first + p * cells : first + (p + 1) * cells,
                        source * samples : (source + 1) * samples,
                    ] = values * gain
        first = side * len(classes) * half * cells
        out[...] = (
            jnp.dot(
                place[first : first + len(classes) * half * cells, :],
                rows[...],
                preferred_element_type=jnp.float32,
            )
            .reshape(out.shape)
            .astype(out.dtype)
        )


def near_body(groups, units, own, core, vis, vis_core, send, keep, place, rows):
    samples = own.shape[1]
    cells = send.shape[2]
    rows[:samples, :] = vis[...]
    for i, u in enumerate(units):
        rows[samples:, i * CHUNK : (i + 1) * CHUNK] = unit(vis_core, u)[...]
    place_and_sum(
        [[listed(own, i, cells), listed(core, i, cells)] for i in range(2)],
        groups,
        place,
        rows,
        send,
        keep,
    )


def plane_body(
    groups, units, own, core, far, relay, vis, vis_core, vis_far, *rest
):
    *vis_relay, send, keep, place, rows = rest
    samples = own.shape[1]
    cells = send.shape[2]
    rows[:samples, :] = vis[...]
    for i, u in enumerate(units):
        rows[samples : 2 * samples, i * CHUNK : (i + 1) * CHUNK] = unit(vis_core, u)[...]
    rows[2 * samples : 3 * samples, :] = vis_far[...]
    each = samples // len(vis_relay)
    for i, piece in enumerate(vis_relay):
        rows[3 * samples + i * each : 3 * samples + (i + 1) * each, :] = piece[...]
    place_and_sum(
        [
            [
                listed(own, 0, cells),
                listed(core, 0, cells),
                listed(far, 0, cells),
                listed(relay, 1, cells),
            ]
        ],
        groups,
        place,
        rows,
        send,
        keep,
    )


def final_body(plan, *refs):
    nchunks = len(plan)
    kept, got = refs[:nchunks], refs[nchunks : 2 * nchunks]
    inv_cov, cos_table, sin_table, out = refs[2 * nchunks :]
    cells = out.shape[2]
    sums = {}
    for units, mine, other in zip(plan, kept, got):
        summed = (mine[...] + other[...].astype(jnp.float32)).astype(jnp.bfloat16)
        for i, u in enumerate(units):
            sums[u] = summed[:, i * CHUNK : (i + 1) * CHUNK]
    cube = jnp.concatenate(
        [
            jnp.concatenate([sums[u] for u in range(part, len(sums), 2)], axis=1)
            for part in range(2)
        ],
        axis=0,
    )
    contract = (((1,), (1,)), ((), ()))
    filtered = lax.dot_general(
        cube, inv_cov[...], contract, preferred_element_type=jnp.float32
    ).astype(jnp.bfloat16)
    cosine = lax.dot_general(cos_table[...], filtered, contract, preferred_element_type=jnp.float32)
    sine = lax.dot_general(sin_table[...], filtered, contract, preferred_element_type=jnp.float32)
    scale = 1.0 / math.sqrt(inv_cov.shape[0])
    out[0] = (cosine[:, :cells] + sine[:, cells:]) * scale
    out[1] = (cosine[:, cells:] - sine[:, :cells]) * scale


def on_device(visibilities, kernel, weights, counts, blocks, inv_cov):
    nblocks = lax.axis_size("chan")
    groups = nblocks // MAXB
    samples, channels = visibilities.shape[1:]
    cells = kernel.shape[2]
    plan = FIRST + LATER
    bf16, f32 = jnp.bfloat16, jnp.float32
    shape = jax.ShapeDtypeStruct
    hbm, anywhere = pl.BlockSpec(memory_space=pltpu.HBM), pl.BlockSpec(memory_space=pl.ANY)
    options = dict(
        compiler_params=pltpu.CompilerParams(vmem_limit_bytes=VMEM_BYTES),
        cost_estimate=pl.CostEstimate(flops=1, bytes_accessed=1, transcendentals=0),
    )

    def swap(values, bit):
        return lax.ppermute(values, "chan", [(i, i ^ bit) for i in range(nblocks)])

    listing = shape((2 * (cells + LABEL_ROWS), samples), bf16)
    operands = (visibilities, kernel, weights, counts, blocks)
    own, core, far, *chunks = pl.pallas_call(
        lambda *refs: prep_body(nblocks, plan, *refs),
        in_specs=[hbm] * 5,
        out_specs=[pl.BlockSpec(memory_space=pltpu.VMEM)] * 3 + [anywhere] * len(plan),
        out_shape=[listing] * 3
        + [shape((samples, len(units) * CHUNK), bf16) for units in plan],
        scratch_shapes=[
            pltpu.VMEM(kernel.shape, bf16),
            pltpu.VMEM(weights.shape, jnp.int32),
            pltpu.VMEM(counts.shape, jnp.int32),
            pltpu.VMEM(blocks.shape, jnp.int32),
            pltpu.SemaphoreType.DMA((4,)),
            pltpu.SemaphoreType.DMA((2 * channels // CHUNK,)),
        ],
        name="prep",
        **options,
    )(*[pltpu.with_memory_space_constraint(x, pltpu.HBM) for x in operands])
    me = lax.axis_index("chan")
    vis_core = swap(visibilities, 1)
    core = swap(core, 1)
    far = swap(far, 2)
    relay = swap(far, 1)

    def grid(body, classes, sources, units, *operands):
        out = (classes, groups // 2, cells, len(units) * CHUNK)
        return pl.pallas_call(
            lambda *refs: body(groups, units, *refs),
            out_shape=[shape(out, bf16), shape(out, f32)],
            scratch_shapes=[
                pltpu.VMEM((classes * groups * cells, sources * samples), bf16),
                pltpu.VMEM((sources * samples, len(units) * CHUNK), bf16),
            ],
            name="grid",
            **options,
        )(*operands)

    def over_planes(send, keep):
        bit = MAXB
        while True:
            arrived = swap(send, bit)
            if keep.shape[1] == 1:
                return keep, arrived
            bit *= 2
            summed = keep + arrived.astype(f32)
            summed = summed.reshape(summed.shape[0], -1, 2, *summed.shape[2:])
            upper = (me // bit) % 2 == 1
            keep = jnp.where(upper, summed[:, :, 1], summed[:, :, 0])
            send = jnp.where(upper, summed[:, :, 0], summed[:, :, 1]).astype(bf16)

    kept, got, sent = [], [], []
    for units, chunk in zip(FIRST, chunks):
        send, keep = grid(near_body, 2, 2, units, own, core, chunk, vis_core)
        keep, arrived = over_planes(send, keep)
        summed = keep[:, 0] + arrived[:, 0].astype(f32)
        kept.append(summed[0])
        got.append(swap(summed[1].astype(bf16), 2))
    for units, chunk in zip(LATER, chunks[len(FIRST) :]):
        vis_far = swap(chunk, 2)
        if sent:
            vis_far, _ = lax.optimization_barrier((vis_far, sent[-1]))
        rows_each = samples // 2
        vis_relay = [swap(vis_far[i * rows_each : (i + 1) * rows_each], 1) for i in range(2)]
        send, keep = grid(
            plane_body, 1, 4, units, own, core, far, relay, chunk, vis_core, vis_far, *vis_relay
        )
        sent.append(send)
        keep, arrived = over_planes(send, keep)
        kept.append(keep[0, 0])
        got.append(arrived[0, 0])
    cos_table, sin_table = delay_tables(channels)
    return pl.pallas_call(
        lambda *refs: final_body(plan, *refs),
        out_shape=shape((2, channels, cells), f32),
        name="transform",
        **options,
    )(*kept, *got, inv_cov, cos_table, sin_table)


def solution(mesh):
    placed = (
        P(None, ("obs", "chan"), None),
        P(None, ("obs", "chan"), None),
        P(("obs", "chan")),
        P(("obs", "chan")),
        P(None, ("obs", "chan")),
        P(),
    )
    return jax.shard_map(
        on_device,
        mesh=mesh,
        in_specs=placed,
        out_specs=P(None, None, ("obs", "chan")),
        check_vma=False,
    )
```

```python
import math

import jax
import jax.numpy as jnp
import numpy as np
from jax import lax
from jax.experimental import pallas as pl
from jax.experimental.pallas import tpu as pltpu
from jax.sharding import PartitionSpec as P

MAXB = 4
LABEL_ROWS = 16
CHUNK = 128
VMEM_BYTES = 48 * 1024 * 1024
PLAN = ((0,), (1, 2, 3), (4, 5))
NEAR = (0,)
DIRECT = (0,)
PIECES = 1
SECOND = (1, 0, 2)
LAST = (2,)
AFTER = {'relay': ['grid0'], 'relay1': ['grid0'], 'relay2': ['grid1'], 'third0': ['grid1', 'grid2', 'second1'], 'second2': ['second0']}


def delay_tables(channels):
    index = np.arange(channels, dtype=np.int64)
    product = index[:, None] * index[None, :] % channels
    angle = product.astype(np.float32) * np.float32(2.0 * math.pi / channels)
    table = np.concatenate([np.cos(angle), np.sin(angle)])
    return jnp.asarray(table.astype(jnp.bfloat16))


def unit(vis, u):
    return vis.at[u % 2, :, pl.ds(u // 2 * CHUNK, CHUNK)]


def prep_body(
    nblocks, vis, kernel_in, weights_in, counts_in, blocks_in, own, core, far, *refs
):
    chunks, (kernel, weights, counts, blocks, sems, cut_sems) = refs[: len(PLAN)], refs[len(PLAN) :]
    copies = [
        pltpu.make_async_copy(source, target, sems.at[i])
        for i, (source, target) in enumerate(
            [(weights_in, weights), (counts_in, counts), (blocks_in, blocks), (kernel_in, kernel)]
        )
    ]
    cuts = [
        pltpu.make_async_copy(unit(vis, u), chunk.at[:, pl.ds(i * CHUNK, CHUNK)], cut_sems.at[u])
        for units, chunk in zip(PLAN, chunks)
        for i, u in enumerate(units)
    ]
    for copy in copies + cuts:
        copy.start()
    for copy in copies:
        copy.wait()
    cells = kernel.shape[2]
    me = lax.axis_index("chan")
    start = blocks[0:1, :]
    weight = weights[...].reshape(1, -1).astype(jnp.float32)
    count = counts[...].reshape(1, -1)
    turned = [kernel[j].astype(jnp.float32).T for j in range(MAXB)]
    picked = []
    for flip in range(MAXB):
        residue = jnp.bitwise_xor(jnp.bitwise_and(me, MAXB - 1), flip)
        which = jnp.bitwise_and(residue - start, MAXB - 1)
        total = None
        for j in range(MAXB):
            gain = jnp.where((which == j) & (j < count), weight, 0.0)
            term = turned[j] * gain
            total = term if total is None else total + term
        label = lax.rem(start + which, nblocks) // MAXB
        picked.append(
            (
                total.astype(jnp.bfloat16),
                jnp.broadcast_to(
                    label.astype(jnp.float32), (LABEL_ROWS, start.shape[1])
                ).astype(jnp.bfloat16),
            )
        )
    for out, flips in ((own, (0, 2)), (core, (1, 3)), (far, (2, 3))):
        for i, flip in enumerate(flips):
            out[i * cells : (i + 1) * cells, :] = picked[flip][0]
            out[2 * cells + i * LABEL_ROWS : 2 * cells + (i + 1) * LABEL_ROWS, :] = picked[flip][1]
    for copy in cuts:
        copy.wait()


def listed(table, i, cells):
    row = 2 * cells + i * LABEL_ROWS
    return table[i * cells : (i + 1) * cells, :], table[row : row + 1, :].astype(jnp.float32)


def grid_body(groups, n, *refs):
    units, near, direct = PLAN[n], n in NEAR, n in DIRECT
    sources = 2 if near else 4
    count = groups if direct else 2
    refs, (place, rows) = refs[:-2], refs[-2:]
    refs, outs = refs[:-count], refs[-count:]
    cells = outs[0].shape[2]
    if near:
        own, core, vis, vis_core = refs
        classes = [[listed(own, i, cells), listed(core, i, cells)] for i in range(2)]
    else:
        own, core, far, relay, vis, vis_core, vis_far, *vis_relay = refs
        classes = [[listed(table, int(i == 3), cells) for i, table in enumerate((own, core, far, relay))]]
    samples = own.shape[1]
    rows[:samples, :] = vis[...]
    for i, u in enumerate(units):
        rows[samples : 2 * samples, i * CHUNK : (i + 1) * CHUNK] = unit(vis_core, u)[...]
    if not near:
        rows[2 * samples : 3 * samples, :] = vis_far[...]
        each = samples // len(vis_relay)
        for i, piece in enumerate(vis_relay):
            rows[3 * samples + i * each : 3 * samples + (i + 1) * each, :] = piece[...]
    plane = lax.axis_index("chan") // MAXB
    if direct:
        wanted = [[jnp.bitwise_xor(plane, away)] for away in range(groups)]
    else:
        bit = jnp.bitwise_and(plane, 1)
        wanted = [[2 * p + side for p in range(groups // 2)] for side in (bit, 1 - bit)]
    first = 0
    for out, blocks in zip(outs, wanted):
        top = first
        for table in classes:
            for block in blocks:
                for source, (values, label) in enumerate(table):
                    gain = jnp.where(label == block.astype(jnp.float32), 1.0, 0.0)
                    place[first : first + cells, source * samples : (source + 1) * samples] = (
                        values * gain.astype(jnp.bfloat16)
                    )
                first += cells
        summed = jnp.dot(place[top:first, :], rows[...], preferred_element_type=jnp.float32)
        out[...] = summed.reshape(out.shape).astype(out.dtype)


def fold_body(tables, inv_cov, folded):
    folded[...] = lax.dot_general(
        tables[...], inv_cov[...], (((1,), (0,)), ((), ())), preferred_element_type=jnp.float32
    ).astype(folded.dtype)


def delay_body(held, last, folded, *refs):
    refs, out = refs[:-1], refs[-1]
    channels, cells = out.shape[1:]
    total = [None, None]
    if last:
        refs, before = refs[:-1], refs[-1]
        total = [before[0], before[1]]
    for i, units in enumerate(held):
        mine, other = refs[2 * i], refs[2 * i + 1]
        summed = (mine[...] + other[...].astype(jnp.float32)).astype(jnp.bfloat16)
        for j, u in enumerate(units):
            part, k = u % 2, u // 2
            both = lax.dot_general(
                folded[:, k * CHUNK : (k + 1) * CHUNK],
                summed[:, j * CHUNK : (j + 1) * CHUNK],
                (((1,), (1,)), ((), ())),
                preferred_element_type=jnp.float32,
            )
            cosine, sine = both[:channels], both[channels:]
            sine = sine if part else -sine
            for half, term in ((part, cosine), (1 - part, sine)):
                total[half] = term if total[half] is None else total[half] + term
    scale = 1.0 / math.sqrt(channels) if last else 1.0
    out[0] = total[0] * scale
    out[1] = total[1] * scale


def on_device(visibilities, kernel, weights, counts, blocks, inv_cov):
    nblocks = lax.axis_size("chan")
    groups = nblocks // MAXB
    samples, channels = visibilities.shape[1:]
    cells = kernel.shape[2]
    bf16, f32 = jnp.bfloat16, jnp.float32
    shape = jax.ShapeDtypeStruct
    hbm, anywhere = pl.BlockSpec(memory_space=pltpu.HBM), pl.BlockSpec(memory_space=pl.ANY)
    options = dict(
        compiler_params=pltpu.CompilerParams(vmem_limit_bytes=VMEM_BYTES),
        cost_estimate=pl.CostEstimate(flops=1, bytes_accessed=1, transcendentals=0),
    )
    made = {}

    def swap(values, bit):
        return lax.ppermute(values, "chan", [(i, i ^ bit) for i in range(nblocks)])

    def tied(name, *values):
        earlier = [made[other] for other in AFTER.get(name, ())]
        return lax.optimization_barrier((*values, *earlier))[: len(values)]

    listing = shape((2 * (cells + LABEL_ROWS), samples), bf16)
    operands = (visibilities, kernel, weights, counts, blocks)
    own, core, far, *chunks = pl.pallas_call(
        lambda *refs: prep_body(nblocks, *refs),
        in_specs=[hbm] * 5,
        out_specs=[pl.BlockSpec(memory_space=pltpu.VMEM)] * 3 + [anywhere] * len(PLAN),
        out_shape=[listing] * 3
        + [shape((samples, len(units) * CHUNK), bf16) for units in PLAN],
        scratch_shapes=[
            pltpu.VMEM(kernel.shape, bf16),
            pltpu.VMEM(weights.shape, jnp.int32),
            pltpu.VMEM(counts.shape, jnp.int32),
            pltpu.VMEM(blocks.shape, jnp.int32),
            pltpu.SemaphoreType.DMA((4,)),
            pltpu.SemaphoreType.DMA((2 * channels // CHUNK,)),
        ],
        name="prep",
        **options,
    )(*[pltpu.with_memory_space_constraint(x, pltpu.HBM) for x in operands])
    me = lax.axis_index("chan")
    vis_core = swap(visibilities, 1)
    core = swap(core, 1)
    far = swap(far, 2)
    vis_far = {n: swap(chunks[n], 2) for n in range(len(PLAN)) if n not in NEAR}

    made.update({f"far{n}": values for n, values in vis_far.items()})

    def grid(n, *operands):
        sources = 2 if n in NEAR else 4
        classes, lanes = 4 // sources, len(PLAN[n]) * CHUNK
        if n in DIRECT:
            out = (classes, 1, cells, lanes)
            outs = [shape(out, f32)] + [shape(out, bf16)] * (groups - 1)
        else:
            out = (classes, groups // 2, cells, lanes)
            outs = [shape(out, f32), shape(out, bf16)]
        keep, *sends = pl.pallas_call(
            lambda *refs: grid_body(groups, n, *refs),
            out_shape=outs,
            scratch_shapes=[
                pltpu.VMEM((classes * groups * cells, sources * samples), bf16),
                pltpu.VMEM((sources * samples, lanes), bf16),
            ],
            name="grid",
            **options,
        )(*operands)
        made[f"grid{n}"] = sends[0]
        sends = tied(f"first{n}", *sends)
        arrived = [swap(send, (i + 1) * MAXB) for i, send in enumerate(sends)]
        made[f"got{n}"] = arrived[0]
        return keep, arrived

    state = {n: grid(n, own, core, chunks[n], vis_core) for n in NEAR}
    (far,) = tied("relay", far)
    relay = swap(far, 1)
    for n in range(len(PLAN)):
        if n in NEAR:
            continue
        (mine,) = tied(f"relay{n}", vis_far[n])
        made[f"mine{n}"] = mine
        each = samples // PIECES
        vis_relay = [swap(mine[i * each : (i + 1) * each], 1) for i in range(PIECES)]
        state[n] = grid(n, own, core, far, relay, chunks[n], vis_core, mine, *vis_relay)

    held = {}
    for n in SECOND:
        keep, arrived = state[n]
        arrived = tied(f"second{n}", *arrived)
        bit = MAXB
        while keep.shape[1] > 1:
            bit *= 2
            summed = keep + arrived[0].astype(f32)
            summed = summed.reshape(summed.shape[0], -1, 2, *summed.shape[2:])
            upper = (me // bit) % 2 == 1
            keep = jnp.where(upper, summed[:, :, 1], summed[:, :, 0])
            send = jnp.where(upper, summed[:, :, 0], summed[:, :, 1]).astype(bf16)
            made[f"second{n}"] = send
            arrived = [swap(send, bit)]
        keep, arrived = keep[:, 0], [piece[:, 0] for piece in arrived]
        if n in NEAR or len(arrived) > 1:
            keep = keep + sum(piece.astype(f32) for piece in arrived[: None if n in NEAR else -1])
            made[f"second{n}"] = keep
        if n in NEAR:
            (send,) = tied(f"third{n}", keep[1].astype(bf16))
            arrived = [swap(send, 2)]
        held[n] = (keep[0], arrived[-1] if n in NEAR else arrived[-1][0])

    tables, early = tied("fold", delay_tables(channels), inv_cov)
    folded = pl.pallas_call(
        fold_body,
        out_shape=shape((2 * channels, channels), bf16),
        name="fold",
        **options,
    )(tables, early)

    def delayed(chosen, last, *extra):
        return pl.pallas_call(
            lambda *refs: delay_body([PLAN[n] for n in chosen], last, *refs),
            out_shape=shape((2, channels, cells), f32),
            name="delay",
            **options,
        )(folded, *[x for n in chosen for x in held[n]], *extra)

    before = delayed([n for n in range(len(PLAN)) if n not in LAST], False)
    return delayed(list(LAST), True, before)


def solution(mesh):
    placed = (
        P(None, ("obs", "chan"), None),
        P(None, ("obs", "chan"), None),
        P(("obs", "chan")),
        P(("obs", "chan")),
        P(None, ("obs", "chan")),
        P(),
    )
    return jax.shard_map(
        on_device,
        mesh=mesh,
        in_specs=placed,
        out_specs=P(None, None, ("obs", "chan")),
        check_vma=False,
    )
```

```python
import math

import jax
import jax.numpy as jnp
import numpy as np
from jax import lax
from jax.experimental import pallas as pl
from jax.experimental.pallas import tpu as pltpu
from jax.sharding import PartitionSpec as P

MAXB = 4
LABEL_ROWS = 16
CHUNK = 128
VMEM_BYTES = 48 * 1024 * 1024
PLAN = ((0,), (1, 2, 3), (4, 5))
NEAR = (0,)
DIRECT = ()
PIECES = 2
SECOND = (1, 0, 2)
LAST = (2,)
AFTER = {'relay1': ['grid0', 'got0'], 'relay2': ['grid1'], 'third0': ['grid1', 'second1'], 'over2': ['core']}


def delay_tables(channels):
    index = np.arange(channels, dtype=np.int64)
    product = index[:, None] * index[None, :] % channels
    angle = product.astype(np.float32) * np.float32(2.0 * math.pi / channels)
    table = np.concatenate([np.cos(angle), np.sin(angle)])
    return jnp.asarray(table.astype(jnp.bfloat16))


def unit(vis, u):
    return vis.at[u % 2, :, pl.ds(u // 2 * CHUNK, CHUNK)]


def prep_body(
    nblocks, vis, kernel_in, weights_in, counts_in, blocks_in, own, core, *refs
):
    chunks, (kernel, weights, counts, blocks, sems, cut_sems) = refs[: len(PLAN)], refs[len(PLAN) :]
    copies = [
        pltpu.make_async_copy(source, target, sems.at[i])
        for i, (source, target) in enumerate(
            [(weights_in, weights), (counts_in, counts), (blocks_in, blocks), (kernel_in, kernel)]
        )
    ]
    cuts = [
        pltpu.make_async_copy(unit(vis, u), chunk.at[:, pl.ds(i * CHUNK, CHUNK)], cut_sems.at[u])
        for units, chunk in zip(PLAN, chunks)
        for i, u in enumerate(units)
    ]
    for copy in copies + cuts:
        copy.start()
    for copy in copies:
        copy.wait()
    cells = kernel.shape[2]
    me = lax.axis_index("chan")
    start = blocks[0:1, :]
    weight = weights[...].reshape(1, -1).astype(jnp.float32)
    count = counts[...].reshape(1, -1)
    turned = [kernel[j].astype(jnp.float32).T for j in range(MAXB)]
    picked = []
    for flip in range(MAXB):
        residue = jnp.bitwise_xor(jnp.bitwise_and(me, MAXB - 1), flip)
        which = jnp.bitwise_and(residue - start, MAXB - 1)
        total = None
        for j in range(MAXB):
            gain = jnp.where((which == j) & (j < count), weight, 0.0)
            term = turned[j] * gain
            total = term if total is None else total + term
        label = lax.rem(start + which, nblocks) // MAXB
        picked.append(
            (
                total.astype(jnp.bfloat16),
                jnp.broadcast_to(
                    label.astype(jnp.float32), (LABEL_ROWS, start.shape[1])
                ).astype(jnp.bfloat16),
            )
        )
    for out, flips in ((own, (0, 2)), (core, (1, 3))):
        for i, flip in enumerate(flips):
            out[i * cells : (i + 1) * cells, :] = picked[flip][0]
            out[2 * cells + i * LABEL_ROWS : 2 * cells + (i + 1) * LABEL_ROWS, :] = picked[flip][1]
    for copy in cuts:
        copy.wait()


def listed(table, i, cells):
    row = 2 * cells + i * LABEL_ROWS
    return table[i * cells : (i + 1) * cells, :], table[row : row + 1, :].astype(jnp.float32)


def grid_body(groups, n, *refs):
    units, near, direct = PLAN[n], n in NEAR, n in DIRECT
    sources = 2 if near else 4
    count = groups if direct else 2
    refs, (place, rows) = refs[:-2], refs[-2:]
    refs, outs = refs[:-count], refs[-count:]
    cells = outs[0].shape[2]
    if near:
        own, core, vis, vis_core = refs
        classes = [[listed(own, i, cells), listed(core, i, cells)] for i in range(2)]
    else:
        own, core, far, vis, vis_core, vis_far, *vis_relay = refs
        held = ((own, 0), (core, 0), (far, 0), (far, 1))
        classes = [[listed(table, i, cells) for table, i in held]]
    samples = own.shape[1]
    rows[:samples, :] = vis[...]
    for i, u in enumerate(units):
        rows[samples : 2 * samples, i * CHUNK : (i + 1) * CHUNK] = unit(vis_core, u)[...]
    if not near:
        rows[2 * samples : 3 * samples, :] = vis_far[...]
        each = samples // len(vis_relay)
        for i, piece in enumerate(vis_relay):
            rows[3 * samples + i * each : 3 * samples + (i + 1) * each, :] = piece[...]
    plane = lax.axis_index("chan") // MAXB
    if direct:
        wanted = [[jnp.bitwise_xor(plane, away)] for away in range(groups)]
    else:
        bit = jnp.bitwise_and(plane, 1)
        wanted = [[2 * p + side for p in range(groups // 2)] for side in (bit, 1 - bit)]
    first = 0
    for out, blocks in zip(outs, wanted):
        top = first
        for table in classes:
            for block in blocks:
                for source, (values, label) in enumerate(table):
                    gain = jnp.where(label == block.astype(jnp.float32), 1.0, 0.0)
                    place[first : first + cells, source * samples : (source + 1) * samples] = (
                        values * gain.astype(jnp.bfloat16)
                    )
                first += cells
        summed = jnp.dot(place[top:first, :], rows[...], preferred_element_type=jnp.float32)
        out[...] = summed.reshape(out.shape).astype(out.dtype)


def fold_body(tables, inv_cov, folded):
    folded[...] = lax.dot_general(
        tables[...], inv_cov[...], (((1,), (0,)), ((), ())), preferred_element_type=jnp.float32
    ).astype(folded.dtype)


def delay_body(held, last, folded, *refs):
    refs, out = refs[:-1], refs[-1]
    channels, cells = out.shape[1:]
    total = [None, None]
    if last:
        refs, before = refs[:-1], refs[-1]
        total = [before[0], before[1]]
    for i, units in enumerate(held):
        mine, other = refs[2 * i], refs[2 * i + 1]
        summed = (mine[...] + other[...].astype(jnp.float32)).astype(jnp.bfloat16)
        for j, u in enumerate(units):
            part, k = u % 2, u // 2
            both = lax.dot_general(
                folded[:, k * CHUNK : (k + 1) * CHUNK],
                summed[:, j * CHUNK : (j + 1) * CHUNK],
                (((1,), (1,)), ((), ())),
                preferred_element_type=jnp.float32,
            )
            cosine, sine = both[:channels], both[channels:]
            sine = sine if part else -sine
            for half, term in ((part, cosine), (1 - part, sine)):
                total[half] = term if total[half] is None else total[half] + term
    scale = 1.0 / math.sqrt(channels) if last else 1.0
    out[0] = total[0] * scale
    out[1] = total[1] * scale


def on_device(visibilities, kernel, weights, counts, blocks, inv_cov):
    nblocks = lax.axis_size("chan")
    groups = nblocks // MAXB
    samples, channels = visibilities.shape[1:]
    cells = kernel.shape[2]
    bf16, f32 = jnp.bfloat16, jnp.float32
    shape = jax.ShapeDtypeStruct
    hbm, anywhere = pl.BlockSpec(memory_space=pltpu.HBM), pl.BlockSpec(memory_space=pl.ANY)
    options = dict(
        compiler_params=pltpu.CompilerParams(vmem_limit_bytes=VMEM_BYTES),
        cost_estimate=pl.CostEstimate(flops=1, bytes_accessed=1, transcendentals=0),
    )
    made = {}

    def swap(values, bit):
        return lax.ppermute(values, "chan", [(i, i ^ bit) for i in range(nblocks)])

    def tied(name, *values):
        earlier = [made[other] for other in AFTER.get(name, ())]
        return lax.optimization_barrier((*values, *earlier))[: len(values)]

    listing = shape((2 * (cells + LABEL_ROWS), samples), bf16)
    operands = (visibilities, kernel, weights, counts, blocks)
    own, core, *chunks = pl.pallas_call(
        lambda *refs: prep_body(nblocks, *refs),
        in_specs=[hbm] * 5,
        out_specs=[pl.BlockSpec(memory_space=pltpu.VMEM)] * 2 + [anywhere] * len(PLAN),
        out_shape=[listing] * 2
        + [shape((samples, len(units) * CHUNK), bf16) for units in PLAN],
        scratch_shapes=[
            pltpu.VMEM(kernel.shape, bf16),
            pltpu.VMEM(weights.shape, jnp.int32),
            pltpu.VMEM(counts.shape, jnp.int32),
            pltpu.VMEM(blocks.shape, jnp.int32),
            pltpu.SemaphoreType.DMA((4,)),
            pltpu.SemaphoreType.DMA((2 * channels // CHUNK,)),
        ],
        name="prep",
        **options,
    )(*[pltpu.with_memory_space_constraint(x, pltpu.HBM) for x in operands])
    me = lax.axis_index("chan")
    vis_core = swap(visibilities, 1)
    core = swap(core, 1)
    tables, label = 2 * cells, 2 * cells + LABEL_ROWS
    far = [x[a:b] for a, b in ((cells, tables), (label, None)) for x in (own, core)]
    far = swap(jnp.concatenate(tied("far", *far)), 2)

    made["far"] = far
    made["core"] = core

    def grid(n, *operands):
        sources = 2 if n in NEAR else 4
        classes, lanes = 4 // sources, len(PLAN[n]) * CHUNK
        if n in DIRECT:
            out = (classes, 1, cells, lanes)
            outs = [shape(out, f32)] + [shape(out, bf16)] * (groups - 1)
        else:
            out = (classes, groups // 2, cells, lanes)
            outs = [shape(out, f32), shape(out, bf16)]
        keep, *sends = pl.pallas_call(
            lambda *refs: grid_body(groups, n, *refs),
            out_shape=outs,
            scratch_shapes=[
                pltpu.VMEM((classes * groups * cells, sources * samples), bf16),
                pltpu.VMEM((sources * samples, lanes), bf16),
            ],
            name="grid",
            **options,
        )(*operands)
        made[f"grid{n}"] = sends[0]
        sends = tied(f"first{n}", *sends)
        arrived = [swap(send, (i + 1) * MAXB) for i, send in enumerate(sends)]
        made[f"got{n}"] = arrived[0]
        return keep, arrived

    state = {n: grid(n, own, core, chunks[n], vis_core) for n in NEAR}
    vis_far = {
        n: swap(tied(f"over{n}", chunks[n])[0], 2) for n in range(len(PLAN)) if n not in NEAR
    }
    made.update({f"far{n}": values for n, values in vis_far.items()})
    for n in range(len(PLAN)):
        if n in NEAR:
            continue
        (mine,) = tied(f"relay{n}", vis_far[n])
        made[f"mine{n}"] = mine
        each = samples // PIECES
        vis_relay = [swap(mine[i * each : (i + 1) * each], 1) for i in range(PIECES)]
        state[n] = grid(n, own, core, far, chunks[n], vis_core, mine, *vis_relay)

    held = {}
    for n in SECOND:
        keep, arrived = state[n]
        arrived = tied(f"second{n}", *arrived)
        bit = MAXB
        while keep.shape[1] > 1:
            bit *= 2
            summed = keep + arrived[0].astype(f32)
            summed = summed.reshape(summed.shape[0], -1, 2, *summed.shape[2:])
            upper = (me // bit) % 2 == 1
            keep = jnp.where(upper, summed[:, :, 1], summed[:, :, 0])
            send = jnp.where(upper, summed[:, :, 0], summed[:, :, 1]).astype(bf16)
            made[f"second{n}"] = send
            arrived = [swap(send, bit)]
            made[f"mid{n}"] = arrived[0]
        keep, arrived = keep[:, 0], [piece[:, 0] for piece in arrived]
        if n in NEAR or len(arrived) > 1:
            keep = keep + sum(piece.astype(f32) for piece in arrived[: None if n in NEAR else -1])
            made[f"second{n}"] = keep
        if n in NEAR:
            (send,) = tied(f"third{n}", keep[1].astype(bf16))
            arrived = [swap(send, 2)]
        held[n] = (keep[0], arrived[-1] if n in NEAR else arrived[-1][0])

    tables, early = tied("fold", delay_tables(channels), inv_cov)
    folded = pl.pallas_call(
        fold_body,
        out_shape=shape((2 * channels, channels), bf16),
        name="fold",
        **options,
    )(tables, early)

    def delayed(chosen, last, *extra):
        return pl.pallas_call(
            lambda *refs: delay_body([PLAN[n] for n in chosen], last, *refs),
            out_shape=shape((2, channels, cells), f32),
            name="delay",
            **options,
        )(folded, *[x for n in chosen for x in held[n]], *extra)

    before = delayed([n for n in range(len(PLAN)) if n not in LAST], False)
    return delayed(list(LAST), True, before)


def solution(mesh):
    placed = (
        P(None, ("obs", "chan"), None),
        P(None, ("obs", "chan"), None),
        P(("obs", "chan")),
        P(("obs", "chan")),
        P(None, ("obs", "chan")),
        P(),
    )
    return jax.shard_map(
        on_device,
        mesh=mesh,
        in_specs=placed,
        out_specs=P(None, None, ("obs", "chan")),
        check_vma=False,
    )
```

```python
import math

import jax
import jax.numpy as jnp
import numpy as np
from jax import lax
from jax.experimental import pallas as pl
from jax.experimental.pallas import tpu as pltpu
from jax.sharding import PartitionSpec as P

MAXB = 4
LABEL_ROWS = 16
CHUNK = 128
VMEM_BYTES = 48 * 1024 * 1024
PLAN = ((0,), (1, 2, 3), (4, 5))
NEAR = (0,)
DIRECT = ()
PIECES = 2
SECOND = (1, 0, 2)
LAST = (2,)
HALVED = (1,)
AFTER = {'relay1': ['grid0', 'got0'], 'relay2': ['grid1'], 'third0': ['grid1', 'second1'], 'over2': ['core'], 'sum0': ['grid1']}


def delay_tables(channels):
    index = np.arange(channels, dtype=np.int64)
    product = index[:, None] * index[None, :] % channels
    angle = product.astype(np.float32) * np.float32(2.0 * math.pi / channels)
    table = np.concatenate([np.cos(angle), np.sin(angle)])
    return jnp.asarray(table.astype(jnp.bfloat16))


def unit(vis, u):
    return vis.at[u % 2, :, pl.ds(u // 2 * CHUNK, CHUNK)]


def prep_body(
    nblocks, vis, kernel_in, weights_in, counts_in, blocks_in, own, core, *refs
):
    chunks, (kernel, weights, counts, blocks, sems, cut_sems) = refs[: len(PLAN)], refs[len(PLAN) :]
    copies = [
        pltpu.make_async_copy(source, target, sems.at[i])
        for i, (source, target) in enumerate(
            [(weights_in, weights), (counts_in, counts), (blocks_in, blocks), (kernel_in, kernel)]
        )
    ]
    cuts = [
        pltpu.make_async_copy(unit(vis, u), chunk.at[:, pl.ds(i * CHUNK, CHUNK)], cut_sems.at[u])
        for units, chunk in zip(PLAN, chunks)
        for i, u in enumerate(units)
    ]
    for copy in copies + cuts:
        copy.start()
    for copy in copies:
        copy.wait()
    cells = kernel.shape[2]
    me = lax.axis_index("chan")
    start = blocks[0:1, :]
    weight = weights[...].reshape(1, -1).astype(jnp.float32)
    count = counts[...].reshape(1, -1)
    turned = [kernel[j].astype(jnp.float32).T for j in range(MAXB)]
    picked = []
    for flip in range(MAXB):
        residue = jnp.bitwise_xor(jnp.bitwise_and(me, MAXB - 1), flip)
        which = jnp.bitwise_and(residue - start, MAXB - 1)
        total = None
        for j in range(MAXB):
            gain = jnp.where((which == j) & (j < count), weight, 0.0)
            term = turned[j] * gain
            total = term if total is None else total + term
        label = lax.rem(start + which, nblocks) // MAXB
        picked.append(
            (
                total.astype(jnp.bfloat16),
                jnp.broadcast_to(
                    label.astype(jnp.float32), (LABEL_ROWS, start.shape[1])
                ).astype(jnp.bfloat16),
            )
        )
    for out, flips in ((own, (0, 2)), (core, (1, 3))):
        for i, flip in enumerate(flips):
            out[i * cells : (i + 1) * cells, :] = picked[flip][0]
            out[2 * cells + i * LABEL_ROWS : 2 * cells + (i + 1) * LABEL_ROWS, :] = picked[flip][1]
    for copy in cuts:
        copy.wait()


def listed(table, i, cells):
    row = 2 * cells + i * LABEL_ROWS
    return table[i * cells : (i + 1) * cells, :], table[row : row + 1, :].astype(jnp.float32)


def grid_body(groups, n, *refs):
    units, near, direct = PLAN[n], n in NEAR, n in DIRECT
    sources = 2 if near else 4
    count = groups if direct else 2
    refs, (place, rows) = refs[:-2], refs[-2:]
    refs, outs = refs[:-count], refs[-count:]
    cells = outs[0].shape[2]
    if near:
        own, core, vis, vis_core = refs
        classes = [[listed(own, i, cells), listed(core, i, cells)] for i in range(2)]
    else:
        own, core, far, vis, vis_core, vis_far, *vis_relay = refs
        held = ((own, 0), (core, 0), (far, 0), (far, 1))
        classes = [[listed(table, i, cells) for table, i in held]]
    samples = own.shape[1]
    rows[:samples, :] = vis[...]
    for i, u in enumerate(units):
        rows[samples : 2 * samples, i * CHUNK : (i + 1) * CHUNK] = unit(vis_core, u)[...]
    if not near:
        rows[2 * samples : 3 * samples, :] = vis_far[...]
        each = samples // len(vis_relay)
        for i, piece in enumerate(vis_relay):
            rows[3 * samples + i * each : 3 * samples + (i + 1) * each, :] = piece[...]
    plane = lax.axis_index("chan") // MAXB
    if direct:
        wanted = [[jnp.bitwise_xor(plane, away)] for away in range(groups)]
    else:
        bit = jnp.bitwise_and(plane, 1)
        wanted = [[2 * p + side for p in range(groups // 2)] for side in (bit, 1 - bit)]
    first = 0
    for out, blocks in zip(outs, wanted):
        top = first
        for table in classes:
            for block in blocks:
                for source, (values, label) in enumerate(table):
                    gain = jnp.where(label == block.astype(jnp.float32), 1.0, 0.0)
                    place[first : first + cells, source * samples : (source + 1) * samples] = (
                        values * gain.astype(jnp.bfloat16)
                    )
                first += cells
        summed = jnp.dot(place[top:first, :], rows[...], preferred_element_type=jnp.float32)
        out[...] = summed.reshape(out.shape).astype(out.dtype)


def fold_body(tables, inv_cov, folded):
    folded[...] = lax.dot_general(
        tables[...], inv_cov[...], (((1,), (0,)), ((), ())), preferred_element_type=jnp.float32
    ).astype(folded.dtype)


def delay_body(held, last, folded, *refs):
    refs, out = refs[:-1], refs[-1]
    channels, cells = out.shape[1:]
    total = [None, None]
    if last:
        refs, before = refs[:-1], refs[-1]
        total = [before[0], before[1]]
    for i, units in enumerate(held):
        mine, other = refs[2 * i], refs[2 * i + 1]
        summed = (mine[...] + other[...].astype(jnp.float32)).astype(jnp.bfloat16)
        for j, u in enumerate(units):
            part, k = u % 2, u // 2
            both = lax.dot_general(
                folded[:, k * CHUNK : (k + 1) * CHUNK],
                summed[:, j * CHUNK : (j + 1) * CHUNK],
                (((1,), (1,)), ((), ())),
                preferred_element_type=jnp.float32,
            )
            cosine, sine = both[:channels], both[channels:]
            sine = sine if part else -sine
            for half, term in ((part, cosine), (1 - part, sine)):
                total[half] = term if total[half] is None else total[half] + term
    scale = 1.0 / math.sqrt(channels) if last else 1.0
    out[0] = total[0] * scale
    out[1] = total[1] * scale


def on_device(visibilities, kernel, weights, counts, blocks, inv_cov):
    nblocks = lax.axis_size("chan")
    groups = nblocks // MAXB
    samples, channels = visibilities.shape[1:]
    cells = kernel.shape[2]
    bf16, f32 = jnp.bfloat16, jnp.float32
    shape = jax.ShapeDtypeStruct
    hbm, anywhere = pl.BlockSpec(memory_space=pltpu.HBM), pl.BlockSpec(memory_space=pl.ANY)
    options = dict(
        compiler_params=pltpu.CompilerParams(vmem_limit_bytes=VMEM_BYTES),
        cost_estimate=pl.CostEstimate(flops=1, bytes_accessed=1, transcendentals=0),
    )
    made = {}

    def swap(values, bit):
        return lax.ppermute(values, "chan", [(i, i ^ bit) for i in range(nblocks)])

    def tied(name, *values):
        earlier = [made[other] for other in AFTER.get(name, ())]
        return lax.optimization_barrier((*values, *earlier))[: len(values)]

    listing = shape((2 * (cells + LABEL_ROWS), samples), bf16)
    operands = (visibilities, kernel, weights, counts, blocks)
    own, core, *chunks = pl.pallas_call(
        lambda *refs: prep_body(nblocks, *refs),
        in_specs=[hbm] * 5,
        out_specs=[pl.BlockSpec(memory_space=pltpu.VMEM)] * 2 + [anywhere] * len(PLAN),
        out_shape=[listing] * 2
        + [shape((samples, len(units) * CHUNK), bf16) for units in PLAN],
        scratch_shapes=[
            pltpu.VMEM(kernel.shape, bf16),
            pltpu.VMEM(weights.shape, jnp.int32),
            pltpu.VMEM(counts.shape, jnp.int32),
            pltpu.VMEM(blocks.shape, jnp.int32),
            pltpu.SemaphoreType.DMA((4,)),
            pltpu.SemaphoreType.DMA((2 * channels // CHUNK,)),
        ],
        name="prep",
        **options,
    )(*[pltpu.with_memory_space_constraint(x, pltpu.HBM) for x in operands])
    me = lax.axis_index("chan")
    vis_core = swap(visibilities, 1)
    core = swap(core, 1)
    made["core"] = core
    angles, early = tied("fold", delay_tables(channels), inv_cov)
    folded = pl.pallas_call(
        fold_body,
        out_shape=shape((2 * channels, channels), bf16),
        name="fold",
        **options,
    )(angles, early)
    made["fold"] = folded
    tables, label = 2 * cells, 2 * cells + LABEL_ROWS
    far = [x[a:b] for a, b in ((cells, tables), (label, None)) for x in (own, core)]
    far = swap(jnp.concatenate(tied("far", *far)), 2)

    made["far"] = far
    made["core"] = core

    def grid(n, *operands):
        sources = 2 if n in NEAR else 4
        classes, lanes = 4 // sources, len(PLAN[n]) * CHUNK
        if n in DIRECT:
            out = (classes, 1, cells, lanes)
            outs = [shape(out, f32)] + [shape(out, bf16)] * (groups - 1)
        else:
            out = (classes, groups // 2, cells, lanes)
            outs = [shape(out, f32), shape(out, bf16)]
        keep, *sends = pl.pallas_call(
            lambda *refs: grid_body(groups, n, *refs),
            out_shape=outs,
            scratch_shapes=[
                pltpu.VMEM((classes * groups * cells, sources * samples), bf16),
                pltpu.VMEM((sources * samples, lanes), bf16),
            ],
            name="grid",
            **options,
        )(*operands)
        made[f"grid{n}"] = sends[0]
        sends = tied(f"first{n}", *sends)
        if n in HALVED:
            halves = jnp.split(sends[0], 2, axis=1)
            arrived = [jnp.concatenate([swap(half, MAXB) for half in halves], axis=1)]
        else:
            arrived = [swap(send, (i + 1) * MAXB) for i, send in enumerate(sends)]
        made[f"got{n}"] = arrived[0]
        return keep, arrived

    state = {n: grid(n, own, core, chunks[n], vis_core) for n in NEAR}
    vis_far = {
        n: swap(tied(f"over{n}", chunks[n])[0], 2) for n in range(len(PLAN)) if n not in NEAR
    }
    made.update({f"far{n}": values for n, values in vis_far.items()})
    for n in range(len(PLAN)):
        if n in NEAR:
            continue
        (mine,) = tied(f"relay{n}", vis_far[n])
        made[f"mine{n}"] = mine
        each = samples // PIECES
        vis_relay = [swap(mine[i * each : (i + 1) * each], 1) for i in range(PIECES)]
        state[n] = grid(n, own, core, far, chunks[n], vis_core, mine, *vis_relay)

    held = {}
    for n in SECOND:
        keep, arrived = state[n]
        arrived = tied(f"second{n}", *arrived)
        bit = MAXB
        while keep.shape[1] > 1:
            bit *= 2
            summed = keep + arrived[0].astype(f32)
            summed = summed.reshape(summed.shape[0], -1, 2, *summed.shape[2:])
            upper = (me // bit) % 2 == 1
            keep = jnp.where(upper, summed[:, :, 1], summed[:, :, 0])
            send = jnp.where(upper, summed[:, :, 0], summed[:, :, 1]).astype(bf16)
            made[f"second{n}"] = send
            arrived = [swap(send, bit)]
            made[f"mid{n}"] = arrived[0]
        arrived = tied(f"sum{n}", *arrived)
        keep, arrived = keep[:, 0], [piece[:, 0] for piece in arrived]
        if n in NEAR or len(arrived) > 1:
            keep = keep + sum(piece.astype(f32) for piece in arrived[: None if n in NEAR else -1])
            made[f"second{n}"] = keep
        if n in NEAR:
            (send,) = tied(f"third{n}", keep[1].astype(bf16))
            arrived = [swap(send, 2)]
            made[f"third{n}"] = arrived[0]
        held[n] = (keep[0], arrived[-1] if n in NEAR else arrived[-1][0])

    def delayed(chosen, last, *extra):
        return pl.pallas_call(
            lambda *refs: delay_body([PLAN[n] for n in chosen], last, *refs),
            out_shape=shape((2, channels, cells), f32),
            name="delay",
            **options,
        )(folded, *[x for n in chosen for x in held[n]], *extra)

    before = delayed([n for n in range(len(PLAN)) if n not in LAST], False)
    return delayed(list(LAST), True, before)


def solution(mesh):
    placed = (
        P(None, ("obs", "chan"), None),
        P(None, ("obs", "chan"), None),
        P(("obs", "chan")),
        P(("obs", "chan")),
        P(None, ("obs", "chan")),
        P(),
    )
    return jax.shard_map(
        on_device,
        mesh=mesh,
        in_specs=placed,
        out_specs=P(None, None, ("obs", "chan")),
        check_vma=False,
    )
```
